32 devices in a mesh: dp: 16 (over z, y, core), tensor: 2 (over x).
Axes of the slice: x: 2, y: 2, z: 4, core: 2. Of those that a mesh axis runs over, the one named last changes fastest.
Arguments:
- hidden_in: bfloat16 [8192, 768], P(('dp', 'tensor')), may hold values from -6 to 6
- attn_gain: float32 [768], replicated, may hold values from 0.5 to 1.5
- qkv_weight: bfloat16 [3, 768, 768], P(None, None, 'tensor'), may hold values from -0.21875 to 0.21875
- out_weight: bfloat16 [768, 768], P('tensor'), may hold values from -1.75 to 1.75
- mlp_gain: float32 [768], replicated, may hold values from 0.5 to 1.5
- in_weight: bfloat16 [2, 768, 1152], P(None, None, 'tensor'), may hold values from -0.21875 to 0.21875
- down_weight: bfloat16 [1152, 768], P('tensor'), may hold values from -0.1875 to 0.1875
- lengths: int32 [16, 4], P('dp'), may hold values from 0 to 512, as said below
- cotangent: bfloat16 [8192, 768], P(('dp', 'tensor')), may hold values from -6 to 6
Outputs:
- layer_out: bfloat16 [8192, 768], P(('dp', 'tensor'))
- grad_input: bfloat16 [8192, 768], P(('dp', 'tensor'))
- grad_attn_gain: float32 [768], replicated
- grad_qkv_weight: float32 [3, 768, 768], P(None, 'dp', 'tensor')
- grad_out_weight: float32 [768, 768], P('tensor', 'dp')
- grad_mlp_gain: float32 [768], replicated
- grad_in_weight: float32 [2, 768, 1152], P(None, 'dp', 'tensor')
- grad_down_weight: float32 [1152, 768], P('tensor', 'dp')
The draws below stay inside these ranges and needn't reach their ends.
Inputs may be any that keep to these rules, and one draw needn't show every extreme that they name: In each row the lengths sum to more than 256 and at most 512; zero is an empty slot. The third sequence of each row begins before slot 256 and ends after it. In every draw one row is a single sequence of 512.
All inputs are finite; a program needn't handle non-finite values.
Results may differ from the reference program's by a relative error of at most 0.018.
Values may be sent and summed in bfloat16 or wider, within the bound.
A program may use at most 128 MiB of HBM per device.

```python
import jax
import jax.numpy as jnp
from jax import lax

D = 768
HEADS = 12
HEAD_DIM = 64
FF = 1152
TOK_DEV = 256
TOK_GRP = 512
GROUPS = 16
TOKENS = 8192


def draw_lengths(key, part):
    key = jax.random.fold_in(key, 7)
    keys = jax.random.split(key, 5)
    totals = jax.random.randint(keys[0], (GROUPS,), TOK_DEV + 1, TOK_GRP + 1)
    middle_start = jax.random.randint(keys[1], (GROUPS,), 0, TOK_DEV)
    middle_end = jax.random.randint(keys[2], (GROUPS,), TOK_DEV + 1, totals + 1)
    leading = jax.random.randint(keys[3], (GROUPS,), 0, middle_start + 1)
    ragged = jnp.stack([leading, middle_start - leading, middle_end - middle_start, totals - middle_end], axis=1)
    full_row = jax.random.randint(keys[4], (), 0, GROUPS)
    single = jnp.array([0, TOK_GRP, 0, 0], dtype=jnp.int32)[jnp.array([0, 0, 1, 0])]
    chosen = jnp.arange(GROUPS, dtype=jnp.int32)[:, None] == full_row
    return jnp.where(chosen, single[None, :], ragged).astype(jnp.int32)


def strengthened(drawn, own_key, source, target, blocks, factor):
    def block_of(dim):
        return (jnp.arange(drawn.shape[dim]) // (drawn.shape[dim] // blocks)).reshape((-1,) + (1,) * (drawn.ndim - 1 - dim))

    one_side = jax.random.permutation(own_key, blocks)[block_of(target)]
    far = (block_of(target) + blocks // 2) % blocks
    return jnp.where((block_of(source) == one_side) | (block_of(source) == far), factor * drawn, drawn)


def block_levels(key, dims, pieces, low, largest):
    level, own = 1.0, jax.random.fold_in(key, 6)
    for dim, parts in pieces:
        heights = jnp.exp(jax.random.uniform(jax.random.fold_in(own, dim), (parts,), jnp.float32, low / len(pieces), largest / len(pieces)))
        level = level * jnp.repeat(heights, dims[dim] // parts).reshape([-1 if axis == dim else 1 for axis in range(len(dims))])
    return level


def bell_draw(key, extent, scale, bound, cuts=(), kind=jnp.bfloat16):
    factor_of = block_levels(key, extent, cuts, -0.22, 0.18) if cuts else 1.0
    result = jax.random.normal(key, extent, jnp.float32) * scale * factor_of
    return jnp.minimum(jnp.maximum(result, -bound), bound).astype(kind)


def gaussian_with(stream_key, extent, deviation, most, cuts, heavy, kind=jnp.bfloat16):
    drawn = deviation * jax.random.normal(stream_key, extent, jnp.float32)
    if cuts:
        drawn = drawn * block_levels(stream_key, extent, cuts, -0.22, 0.18)
    return jnp.clip(strengthened(drawn, jax.random.fold_in(stream_key, 3), *heavy), -most, most).astype(kind)


def setup_inputs(seed: int = 0) -> dict:
    key_list = jax.random.split(jax.random.key(seed), 10)
    hidden_in = bell_draw(key_list[0], (TOKENS, D), 1.0, 6.0, ((0, 32),))
    attn_gain = jnp.clip(1.0 + 0.1 * jax.random.normal(key_list[1], (D,), jnp.float32), 0.5, 1.5)
    qkv_weight = bell_draw(key_list[2], (3, D, HEADS * HEAD_DIM), D ** -0.5, 0.21875, ((2, 2),))
    out_weight = bell_draw(key_list[3], (HEADS * HEAD_DIM, D), (HEADS * HEAD_DIM // 64) ** -0.5, 1.75, ((0, 2),))
    mlp_gain = jnp.clip(1.0 + 0.1 * jax.random.normal(key_list[4], (D,), jnp.float32), 0.5, 1.5)
    in_weight = bell_draw(key_list[5], (2, D, FF), D ** -0.5, 0.21875, ((2, 2),))
    down_weight = bell_draw(key_list[6], (FF, D), FF ** -0.5, 0.1875, ((0, 2),))
    lengths = draw_lengths(jax.random.fold_in(key_list[9], 71), 0)
    cotangent = gaussian_with(key_list[8], (TOKENS, D), 1.0, 6.0, ((0, 32),), (0, 1, 32, 2.75))
    return {"hidden_in": hidden_in, "attn_gain": attn_gain, "qkv_weight": qkv_weight, "out_weight": out_weight, "mlp_gain": mlp_gain, "in_weight": in_weight, "down_weight": down_weight, "lengths": lengths, "cotangent": cotangent}


EPSILON = 1e-05
ROPE_BASE = 160000.0
PRECISE = lax.Precision.HIGHEST

@jax.custom_vjp
def low(v):
    return lax.optimization_barrier(v.astype(jnp.bfloat16)).astype(jnp.float32)

@jax.custom_vjp
def low_back(v):
    return v

def low_keep(v):
    return (low(v), None)

def low_pass(kept, grad):
    return (grad,)

def back_keep(v):
    return (v, None)

def back_low(kept, grad):
    return (low(grad),)
low.defvjp(low_keep, low_pass)
low_back.defvjp(back_keep, back_low)

def positions(lengths_row, slot_count):
    token_index = jnp.arange(slot_count, dtype=jnp.int32)
    cumulative = jnp.cumsum(lengths_row).astype(jnp.int32)
    segment = lax.optimization_barrier(jnp.sum((token_index[:, None] >= cumulative[None, :]).astype(jnp.int32), axis=1)).astype(jnp.int32)
    bounds = jnp.concatenate([(cumulative - lengths_row).astype(jnp.int32), cumulative[-1:]])
    pick_slot = segment[:, None] == jnp.arange(bounds.shape[0], dtype=jnp.int32)[None, :]
    doc_start = lax.optimization_barrier(jnp.sum(jnp.where(pick_slot, bounds[None, :], 0), axis=1)).astype(jnp.int32)
    return (segment, token_index - doc_start)

def rope_tables(position, head_width):
    half_dim = head_width // 2
    frequency = ROPE_BASE ** (-(2.0 * jnp.arange(half_dim, dtype=jnp.float32)) / head_width)
    angles = position.astype(jnp.float32)[:, None] * frequency[None, :]
    return (jnp.cos(angles), jnp.sin(angles))

def rotate(field, cosine, sine_table):
    half_dim = field.shape[-1] // 2
    first_half = field[..., :half_dim]
    second_half = field[..., half_dim:]
    cos_part = cosine[:, None, :]
    sin_part = sine_table[:, None, :]
    return jnp.concatenate([first_half * cos_part - second_half * sin_part, second_half * cos_part + first_half * sin_part], axis=-1)

def layer_norm(field, gain_vec):
    centred = field - lax.optimization_barrier(jnp.mean(field, axis=-1, keepdims=True))
    variance = lax.optimization_barrier(jnp.mean(centred * centred, axis=-1, keepdims=True))
    return centred * lax.rsqrt(variance + EPSILON) * gain_vec

def forward(group_x, attn_gain, qkv_weight, out_weight, mlp_gain, in_weight, down_weight, segment, cosine, sine_table):
    tokens_n = group_x.shape[0]
    head_shape = (tokens_n, HEADS, HEAD_DIM)
    normed = low(layer_norm(group_x, attn_gain))
    qkv = low_back(jnp.einsum('td,cde->cte', normed, qkv_weight, precision=PRECISE))
    queries = low(rotate(qkv[0].reshape(head_shape), cosine, sine_table))
    key_rows = low(rotate(qkv[1].reshape(head_shape), cosine, sine_table))
    value_rows = low(qkv[2].reshape(head_shape))
    scores = low_back(jnp.einsum('qhd,khd->hqk', queries, key_rows, precision=PRECISE) * HEAD_DIM ** (-0.5))
    same_doc = segment[:, None] == segment[None, :]
    scores = jnp.where(same_doc[None], scores, -jnp.inf)
    attn_probs = low(jax.nn.softmax(scores, axis=-1))
    attended = jnp.einsum('hqk,khd->qhd', attn_probs, value_rows, precision=PRECISE).reshape(tokens_n, HEADS * HEAD_DIM)
    attended = low_back(low(attended))
    branch = low_back(jnp.dot(attended, out_weight, precision=PRECISE))
    middle = group_x + branch
    normed_two = low(layer_norm(middle, mlp_gain))
    gate_up = low_back(jnp.einsum('td,cdf->ctf', normed_two, in_weight, precision=PRECISE))
    hidden = low(jax.nn.gelu(gate_up[0], approximate=False) * gate_up[1])
    branch_two = low_back(jnp.dot(hidden, down_weight, precision=PRECISE))
    return middle + branch_two

def reference(hidden_in, attn_gain, qkv_weight, out_weight, mlp_gain, in_weight, down_weight, lengths, cotangent):
    params = tuple((array_in.astype(jnp.float32) for array_in in (attn_gain, qkv_weight, out_weight, mlp_gain, in_weight, down_weight)))
    inputs_all = hidden_in.astype(jnp.float32).reshape(GROUPS, TOK_GRP, D)
    cotangents = cotangent.astype(jnp.float32).reshape(GROUPS, TOK_GRP, D)

    def one_group(running, group_item):
        group_x, group_dy, lengths_row = group_item
        segment, position = positions(lengths_row, TOK_GRP)
        cosine, sine_table = rope_tables(position, HEAD_DIM)

        def run(field, p_one, p_two, p_three, p_four, p_five, p_six):
            return forward(field, p_one, p_two, p_three, p_four, p_five, p_six, segment, cosine, sine_table)
        output, pullback = jax.vjp(run, group_x, *params)
        gradients = pullback(group_dy)
        running = tuple((accum + update for accum, update in zip(running, gradients[1:])))
        return (running, (output.astype(jnp.bfloat16), gradients[0].astype(jnp.bfloat16)))
    initial = tuple((jnp.zeros(weight.shape, jnp.float32) for weight in params))
    summed, (outputs_all, grads_in) = lax.scan(one_group, initial, (inputs_all, cotangents, lengths))
    return (outputs_all.reshape(TOKENS, D), grads_in.reshape(TOKENS, D), summed[0], summed[1], summed[2], summed[3], summed[4], summed[5])
```

```python
import functools

import jax
import jax.numpy as jnp
from jax import lax
from jax.experimental import pallas as pl
from jax.experimental.pallas import tpu as pltpu
from jax.sharding import PartitionSpec as P

HEAD_DIM = 64


EPSILON = 1e-05
ROPE_BASE = 160000.0


def positions(lengths_row, slot_count):
    token_index = jnp.arange(slot_count, dtype=jnp.int32)
    cumulative = jnp.cumsum(lengths_row)
    segment = jnp.sum((token_index[:, None] >= cumulative[None, :]).astype(jnp.int32), axis=1)
    bounds = jnp.concatenate([cumulative - lengths_row, cumulative[-1:]])
    pick_slot = segment[:, None] == jnp.arange(bounds.shape[0], dtype=jnp.int32)[None, :]
    doc_start = jnp.sum(jnp.where(pick_slot, bounds[None, :], 0), axis=1)
    return (segment, token_index - doc_start)


def rope_tables(position, head_width):
    half_dim = head_width // 2
    frequency = ROPE_BASE ** (-(2.0 * jnp.arange(half_dim, dtype=jnp.float32)) / head_width)
    angles = position.astype(jnp.float32)[:, None] * frequency[None, :]
    return (jnp.cos(angles), jnp.sin(angles))


def rotate(field, cosine, sine_table):
    half_dim = field.shape[-1] // 2
    first_half = field[..., :half_dim]
    second_half = field[..., half_dim:]
    cos_part = cosine[:, None, :]
    sin_part = sine_table[:, None, :]
    return jnp.concatenate(
        [
            first_half * cos_part - second_half * sin_part,
            second_half * cos_part + first_half * sin_part,
        ],
        axis=-1,
    )


def norm_parts(field, gain_vec):
    centred = field - jnp.mean(field, axis=-1, keepdims=True)
    variance = jnp.mean(centred * centred, axis=-1, keepdims=True)
    inv_std = lax.rsqrt(variance + EPSILON)
    standard = centred * inv_std
    return (standard * gain_vec, standard, inv_std)


def norm_back(gradient, gain_vec, standard, inv_std):
    scaled = gradient * gain_vec
    return inv_std * (
        scaled
        - jnp.mean(scaled, axis=-1, keepdims=True)
        - standard * jnp.mean(scaled * standard, axis=-1, keepdims=True)
    )


def gelu_exact(field):
    return jax.nn.gelu(field, approximate=False)


def partner_of(place, bit):
    side = (place // (1 << bit)) % 2
    return place + (1 - 2 * side) * (1 << bit), side


def halving_kernel(bits, count, *refs):
    parts, gains = refs[:count], refs[count]
    outs, gains_out = refs[count + 1 : 2 * count + 1], refs[2 * count + 1]
    scratch = refs[2 * count + 2 :]
    landed = [scratch[c * bits : (c + 1) * bits] for c in range(count)]
    gain_land, gain_sum, send_sem, recv_sem, gain_send, gain_recv = scratch[count * bits :]
    me = lax.axis_index("dp")
    across = 1 - lax.axis_index("tensor")
    pairs = [partner_of(me, b) for b in range(bits)]
    targets = [{"dp": p} for p, _ in pairs] + [{"tensor": across}]

    barrier = pltpu.get_barrier_semaphore()
    for target in targets:
        pl.semaphore_signal(barrier, inc=1, device_id=target, device_id_type=pl.DeviceIdType.MESH)
    pl.semaphore_wait(barrier, bits + 1)

    def held(c, step):
        return parts[c] if step == 0 else landed[c][step - 1]

    def copy_of(c, step):
        lead = (slice(None),) * (bits - step - 1)
        return pltpu.make_async_remote_copy(
            src_ref=held(c, step).at[lead + (1 - pairs[step][1],)],
            dst_ref=landed[c][step],
            send_sem=send_sem.at[c, step],
            recv_sem=recv_sem.at[c, step],
            device_id=targets[step],
            device_id_type=pl.DeviceIdType.MESH,
        )

    def gain_copy(step):
        return pltpu.make_async_remote_copy(
            src_ref=gains if step == 0 else gain_sum.at[step - 1],
            dst_ref=gain_land.at[step],
            send_sem=gain_send.at[step],
            recv_sem=gain_recv.at[step],
            device_id=targets[step],
            device_id_type=pl.DeviceIdType.MESH,
        )

    def finish(c, step):
        copy_of(c, step).wait_recv()
        side = pairs[step][1]
        dims = bits - step - 1
        last = step == bits - 1

        def add(i, _):
            at = tuple((i // (1 << (dims - 1 - d))) % 2 for d in range(dims))
            total = landed[c][step][at].astype(jnp.float32) + held(c, step)[at + (side,)].astype(
                jnp.float32
            )
            if last:
                outs[c][...] = total
            else:
                landed[c][step][at] = total.astype(jnp.bfloat16)
            return 0

        if last:
            add(0, 0)
        else:
            lax.fori_loop(0, 1 << dims, add, 0)

    def finish_gain(step):
        gain_copy(step).wait_recv()
        before = gains[...] if step == 0 else gain_sum[step - 1]
        if step == bits:
            gains_out[...] = before + gain_land[step]
        else:
            gain_sum[step] = before + gain_land[step]

    for tick in range(max(count, 2) + bits):
        for step in range(bits, -1, -1):
            c = tick - step
            if 0 <= c < count:
                if step > 0:
                    finish(c, step - 1)
                if step < bits:
                    copy_of(c, step).start()
        if 0 < tick <= bits + 1:
            finish_gain(tick - 1)
        if tick <= bits:
            gain_copy(tick).start()
    for c in range(count):
        for step in range(bits):
            copy_of(c, step).wait_send()
    for step in range(bits + 1):
        gain_copy(step).wait_send()


def reduce_over_groups(grads, gains):
    groups = lax.axis_size("dp")
    bits = groups.bit_length() - 1
    rows = grads[0].shape[0] // groups
    padded = -(-rows // 16) * 16
    blocks = []
    for grad in grads:
        block = grad.astype(jnp.bfloat16).reshape(groups, rows, grad.shape[1])
        if padded != rows:
            block = jnp.pad(block, ((0, 0), (0, padded - rows), (0, 0)))
        blocks.append(block.reshape((2,) * bits + (padded, grad.shape[1])))
    count = len(grads)
    vmem = pl.BlockSpec(memory_space=pltpu.VMEM)
    scratch = [
        pltpu.VMEM((2,) * (bits - step - 1) + (padded, grad.shape[1]), jnp.bfloat16)
        for grad in grads
        for step in range(bits)
    ]
    results = pl.pallas_call(
        functools.partial(halving_kernel, bits, count),
        out_shape=[jax.ShapeDtypeStruct((padded, g.shape[1]), jnp.float32) for g in grads]
        + [jax.ShapeDtypeStruct(gains.shape, jnp.float32)],
        in_specs=[vmem] * (count + 1),
        out_specs=[vmem] * (count + 1),
        scratch_shapes=scratch
        + [
            pltpu.VMEM((bits + 1,) + gains.shape, jnp.float32),
            pltpu.VMEM((bits,) + gains.shape, jnp.float32),
            pltpu.SemaphoreType.DMA((count, bits)),
            pltpu.SemaphoreType.DMA((count, bits)),
            pltpu.SemaphoreType.DMA((bits + 1,)),
            pltpu.SemaphoreType.DMA((bits + 1,)),
        ],
        compiler_params=pltpu.CompilerParams(
            collective_id=0, has_side_effects=True, vmem_limit_bytes=48 * 1024 * 1024
        ),
    )(*blocks, gains)
    return [r[:rows] for r in results[:count]], results[count]


def on_device(
    hidden_in,
    attn_gain,
    qkv_weight,
    out_weight,
    mlp_gain,
    in_weight,
    down_weight,
    lengths,
    cotangent,
):
    tok_rows = hidden_in.shape[0]
    tok_group = tok_rows * lax.axis_size("tensor")
    local_width = qkv_weight.shape[2]
    head_shape = (tok_group, local_width // HEAD_DIM, HEAD_DIM)
    score_scale = HEAD_DIM ** (-0.5)
    segment, position = positions(lengths[0], tok_group)
    cosine, sine_table = rope_tables(position, HEAD_DIM)
    same_doc = (segment[:, None] == segment[None, :])[None]
    inputs_f = hidden_in.astype(jnp.float32)
    normed, standard_one, inv_one = norm_parts(inputs_f, attn_gain)
    normed_b = normed.astype(jnp.bfloat16)
    full_one = lax.all_gather(normed_b, "tensor", axis=0, tiled=True)
    qkv = jnp.einsum("td,cde->cte", full_one, qkv_weight, preferred_element_type=jnp.float32)
    queries = rotate(qkv[0].reshape(head_shape), cosine, sine_table).astype(jnp.bfloat16)
    key_rows = rotate(qkv[1].reshape(head_shape), cosine, sine_table).astype(jnp.bfloat16)
    value_rows = qkv[2].reshape(head_shape).astype(jnp.bfloat16)
    scores = (
        jnp.einsum("qhd,khd->hqk", queries, key_rows, preferred_element_type=jnp.float32)
        * score_scale
    )
    scores = jnp.where(same_doc, scores, -jnp.inf)
    row_peak = jnp.max(scores, axis=-1, keepdims=True)
    exponent = jnp.exp(scores - row_peak)
    row_total = jnp.sum(exponent, axis=-1, keepdims=True)
    logsum = row_peak + jnp.log(row_total)
    probs_b = (exponent / row_total).astype(jnp.bfloat16)
    attended = (
        jnp.einsum("hqk,khd->qhd", probs_b, value_rows, preferred_element_type=jnp.float32)
        .reshape(tok_group, local_width)
        .astype(jnp.bfloat16)
    )
    rows_in = attended
    branch = lax.psum_scatter(
        jnp.dot(rows_in, out_weight, preferred_element_type=jnp.float32).astype(jnp.bfloat16),
        "tensor",
        scatter_dimension=0,
        tiled=True,
    ).astype(jnp.float32)
    middle = inputs_f + branch
    normed_two, standard_two, inv_two = norm_parts(middle, mlp_gain)
    normed_two_b = normed_two.astype(jnp.bfloat16)
    full_two = lax.all_gather(normed_two_b, "tensor", axis=0, tiled=True)
    gate_up = jnp.einsum("td,cdf->ctf", full_two, in_weight, preferred_element_type=jnp.float32)
    active, gelu_pull = jax.vjp(gelu_exact, gate_up[0])
    hidden_b = (active * gate_up[1]).astype(jnp.bfloat16)
    rows_in = hidden_b
    branch_two = lax.psum_scatter(
        jnp.dot(rows_in, down_weight, preferred_element_type=jnp.float32).astype(jnp.bfloat16),
        "tensor",
        scatter_dimension=0,
        tiled=True,
    ).astype(jnp.float32)
    layer_out = (middle + branch_two).astype(jnp.bfloat16)
    grad_out = cotangent.astype(jnp.float32)
    grad_rows = lax.all_gather(cotangent, "tensor", axis=0, tiled=True)
    grad_down = lax.dot_general(
        grad_rows, hidden_b, (((0,), (0,)), ((), ())), preferred_element_type=jnp.float32
    )
    grad_hidden = lax.dot_general(
        grad_rows, down_weight, (((1,), (1,)), ((), ())), preferred_element_type=jnp.float32
    )
    grad_up = grad_hidden * active
    grad_gate = gelu_pull(grad_hidden * gate_up[1])[0]
    grad_gate_up = jnp.stack([grad_gate, grad_up]).astype(jnp.bfloat16)
    grad_in = jnp.einsum("td,ctf->cdf", full_two, grad_gate_up, preferred_element_type=jnp.float32)
    rows_in = grad_gate_up
    grad_normed_two = lax.psum_scatter(
        jnp.einsum("ctf,cdf->td", rows_in, in_weight, preferred_element_type=jnp.float32).astype(
            jnp.bfloat16
        ),
        "tensor",
        scatter_dimension=0,
        tiled=True,
    ).astype(jnp.float32)
    gain_two_part = jnp.sum(grad_normed_two * standard_two, axis=0)
    grad_middle = grad_out + norm_back(grad_normed_two, mlp_gain, standard_two, inv_two)
    grad_middle_b = grad_middle.astype(jnp.bfloat16)
    branch_grads = lax.all_gather(grad_middle_b, "tensor", axis=0, tiled=True)
    grad_wout = lax.dot_general(
        branch_grads, attended, (((0,), (0,)), ((), ())), preferred_element_type=jnp.float32
    )
    grad_attended = (
        lax.dot_general(
            branch_grads, out_weight, (((1,), (1,)), ((), ())), preferred_element_type=jnp.float32
        )
        .astype(jnp.bfloat16)
        .reshape(head_shape)
    )
    raw_scores = (
        jnp.einsum("qhd,khd->hqk", queries, key_rows, preferred_element_type=jnp.float32)
        * score_scale
    )
    attn_probs = jnp.where(same_doc, jnp.exp(raw_scores - logsum), 0.0)
    grad_probs = jnp.einsum(
        "qhd,khd->hqk", grad_attended, value_rows, preferred_element_type=jnp.float32
    )
    grad_values = jnp.einsum(
        "hqk,qhd->khd",
        attn_probs.astype(jnp.bfloat16),
        grad_attended,
        preferred_element_type=jnp.float32,
    )
    inner_sum = jnp.sum(attn_probs * grad_probs, axis=-1, keepdims=True)
    grad_scores = (attn_probs * (grad_probs - inner_sum)).astype(jnp.bfloat16)
    grad_queries = (
        jnp.einsum("hqk,khd->qhd", grad_scores, key_rows, preferred_element_type=jnp.float32)
        * score_scale
    )
    grad_keys = (
        jnp.einsum("hqk,qhd->khd", grad_scores, queries, preferred_element_type=jnp.float32)
        * score_scale
    )
    grad_qkv = jnp.stack(
        [
            rotate(grad_queries, cosine, -sine_table).reshape(tok_group, local_width),
            rotate(grad_keys, cosine, -sine_table).reshape(tok_group, local_width),
            grad_values.reshape(tok_group, local_width),
        ]
    ).astype(jnp.bfloat16)
    grad_wqkv = jnp.einsum("td,cte->cde", full_one, grad_qkv, preferred_element_type=jnp.float32)
    rows_in = grad_qkv
    grad_normed_one = lax.psum_scatter(
        jnp.einsum("cte,cde->td", rows_in, qkv_weight, preferred_element_type=jnp.float32).astype(
            jnp.bfloat16
        ),
        "tensor",
        scatter_dimension=0,
        tiled=True,
    ).astype(jnp.float32)
    gain_one_part = jnp.sum(grad_normed_one * standard_one, axis=0)
    grad_input = (
        grad_middle + norm_back(grad_normed_one, attn_gain, standard_one, inv_one)
    ).astype(jnp.bfloat16)
    gains = jnp.concatenate(
        [gain_one_part[None], gain_two_part[None], jnp.zeros((6, gain_one_part.shape[0]), jnp.float32)]
    )
    sums, gains = reduce_over_groups(
        [grad_in[0], grad_in[1], grad_down, grad_wout, grad_wqkv[0], grad_wqkv[1], grad_wqkv[2]], gains
    )
    gain_one, gain_two = gains[0], gains[1]
    summed_in = jnp.stack(sums[:2])
    summed_down = sums[2].T
    summed_out = sums[3].T
    summed_qkv = jnp.stack(sums[4:])
    return (
        layer_out,
        grad_input,
        gain_one,
        summed_qkv,
        summed_out,
        gain_two,
        summed_in,
        summed_down,
    )


def solution(mesh):
    return jax.shard_map(
        on_device,
        mesh=mesh,
        in_specs=(
            P(("dp", "tensor"), None),
            P(),
            P(None, None, "tensor"),
            P("tensor", None),
            P(),
            P(None, None, "tensor"),
            P("tensor", None),
            P("dp", None),
            P(("dp", "tensor"), None),
        ),
        out_specs=(
            P(("dp", "tensor"), None),
            P(("dp", "tensor"), None),
            P(),
            P(None, "dp", "tensor"),
            P("tensor", "dp"),
            P(),
            P(None, "dp", "tensor"),
            P("tensor", "dp"),
        ),
        check_vma=False,
    )
```
